32 devices in a mesh: groups: 2 (over y), adapter: 4 (over z), tensor: 2 (over x), sub: 2 (over core).
Axes of the slice: x: 2, y: 2, z: 4, core: 2. Of those that a mesh axis runs over, the one named last changes fastest.
Arguments:
- hidden: bfloat16 [2048, 4, 8192], P(('groups', 'adapter'), None, 'tensor'), parts along dimension 0, may hold values from -6 to 6
- request_adapter: int32 [2048], P(('groups', 'adapter')), parts along dimension 0, may hold values from 0 to 63, as said below
- value_matrix: bfloat16 [8192, 1024], P('tensor', 'sub'), may hold values from -0.0625 to 0.0625
- adapter_down: bfloat16 [64, 8192, 64], P('adapter', ('tensor', 'sub')), may hold values from -0.0625 to 0.0625
- adapter_up: bfloat16 [64, 64, 1024], P('adapter', None, 'sub'), may hold values from -0.75 to 0.75
Outputs:
- projected: bfloat16 [2048, 4, 1024], P(('groups', 'adapter'), None, 'sub'), parts along dimension 0
The draws below stay inside these ranges and needn't reach their ends.
There are 2 independent parts, one for each index of `groups`. The reference program is written for one: setup_inputs(seed, part) draws one part's arguments, and reference() takes and returns one part's arrays. A program takes and returns all parts, laid end to end along the dimension named above; an argument that names none is the same for every part. Nothing has to cross between parts.
Inputs may be any that keep to these rules, and one draw needn't show every extreme that they name: The adapter of request r is held by index request_adapter[r] // 16 of adapter. Among the 256 requests of one index of adapter (aligned blocks), at most 128 have adapters held by the same index; in every draw some index holds the adapters of exactly 128 requests of every block.
All inputs are finite; a program needn't handle non-finite values.
Results may differ from the reference program's by a relative error of at most 0.005.
Values may be sent and summed in bfloat16 or wider, within the bound.
A program may use at most 128 MiB of HBM per device.

```python
import math
import jax
import jax.numpy as jnp
from jax import lax

MODEL_WIDTH = 8192
VALUE_WIDTH = 1024
ADAPTER_RANK = 64
STEPS = 4
ADAPT_DEV = 16
REQS = 1024
ADAPTER_TOTAL = 64
CAP = 128


def draw_request_adapter(key, part):
    key = jax.random.fold_in(key, 7)
    owner_count = ADAPTER_TOTAL // ADAPT_DEV
    per_block = REQS // owner_count
    capacity = CAP
    key_hot, key_rest = jax.random.split(key)
    hot_owner = jax.random.randint(key_hot, (), 0, owner_count)
    other_owners = (hot_owner + 1 + jnp.arange(owner_count - 1)) % owner_count

    def one_block(block_key):
        key_cells, key_shuffle, key_local = jax.random.split(block_key, 3)
        chosen_cells = jax.random.permutation(key_cells, (owner_count - 1) * capacity)[:per_block - capacity]
        owner_of = jnp.concatenate([jnp.full((capacity,), hot_owner, jnp.int32), other_owners[chosen_cells // capacity].astype(jnp.int32)])
        shuffle = jax.random.permutation(key_shuffle, per_block)
        owner_of = owner_of[shuffle]
        local_id = jax.random.randint(key_local, (per_block,), 0, ADAPT_DEV)
        return (owner_of * ADAPT_DEV + local_id).astype(jnp.int32)
    block_keys = jax.random.split(key_rest, owner_count)
    return jax.vmap(one_block)(block_keys).reshape(REQS)


def block_scale(rng, shape, shards, smallest, top_value):
    def one(dim, parts):
        steps = jax.random.uniform(jax.random.fold_in(jax.random.fold_in(rng, 6), dim), (parts,), jnp.float32, smallest / len(shards), top_value / len(shards))
        return jnp.repeat(jnp.exp(steps), shape[dim] // parts).reshape((-1,) + (1,) * (len(shape) - dim - 1))

    factor_of = one(*shards[0])
    for cut in shards[1:]:
        factor_of = factor_of * one(*cut)
    return factor_of


def bell_draw(rng, extent, spread, bound, cuts=(), held_as=jnp.bfloat16):
    entries = spread * jax.random.normal(rng, extent, jnp.float32)
    if cuts:
        entries = entries * block_scale(rng, extent, cuts, -0.22, 0.18)
    return jnp.clip(entries, -bound, bound).astype(held_as)


def setup_inputs(seed: int = 0, part: int = 0) -> dict:
    splits = jax.random.split(jax.random.key(seed), 6)
    own_keys = jax.random.split(jax.random.fold_in(splits[5], part), 6)
    return {
        "hidden": bell_draw(own_keys[0], (REQS, STEPS, MODEL_WIDTH), 1.0, 6.0, ((0, 4), (2, 2))),
        "request_adapter": draw_request_adapter(jax.random.fold_in(jax.random.fold_in(splits[5], part), 71), part),
        "value_matrix": bell_draw(splits[2], (MODEL_WIDTH, VALUE_WIDTH), MODEL_WIDTH ** -0.5, 0.0625, ((0, 2), (1, 2))),
        "adapter_down": bell_draw(splits[3], (ADAPTER_TOTAL, MODEL_WIDTH, ADAPTER_RANK), MODEL_WIDTH ** -0.5, 0.0625, ((0, 4), (1, 4))),
        "adapter_up": bell_draw(splits[4], (ADAPTER_TOTAL, ADAPTER_RANK, VALUE_WIDTH), ADAPTER_RANK ** -0.5, 0.75, ((0, 4), (2, 2))),
    }


adapter_scale = 0.5


def reference(hidden, request_adapter, value_matrix, adapter_down, adapter_up):
    plain_rows = jnp.dot(hidden.reshape(REQS * STEPS, MODEL_WIDTH), value_matrix, preferred_element_type=jnp.float32)
    plain_rows = plain_rows.reshape(REQS, STEPS, VALUE_WIDTH)
    group = math.gcd(REQS, 32)

    def one_block(blocked):
        rows_in, incoming_index = blocked
        down_matrices = adapter_down[incoming_index].astype(jnp.float32)
        reduced_rows = jnp.einsum("rsd,rdk->rsk", rows_in.astype(jnp.float32), down_matrices, precision=lax.Precision.HIGHEST)
        up_matrices = adapter_up[incoming_index].astype(jnp.float32)
        return jnp.einsum("rsk,rkc->rsc", reduced_rows, up_matrices, precision=lax.Precision.HIGHEST)

    update_rows = lax.map(one_block, (hidden.reshape(REQS // group, group, STEPS, MODEL_WIDTH), request_adapter.reshape(REQS // group, group)))
    update_rows = update_rows.reshape(REQS, STEPS, VALUE_WIDTH)
    return (plain_rows + adapter_scale * update_rows).astype(jnp.bfloat16)
```

```python
import functools

import jax
import jax.numpy as jnp
from jax import lax
from jax.experimental import pallas as pl
from jax.experimental.pallas import tpu as pltpu
from jax.sharding import PartitionSpec as P

adapter_scale = 0.5


def widen_rows(reduced_rows, up_table, group_lengths):
    high_part = reduced_rows.astype(jnp.bfloat16)
    low_part = (reduced_rows - high_part.astype(jnp.float32)).astype(jnp.bfloat16)
    first = lax.ragged_dot(high_part, up_table, group_lengths, preferred_element_type=jnp.float32)
    second = lax.ragged_dot(low_part, up_table, group_lengths, preferred_element_type=jnp.float32)
    return first + second


def routed(hidden, request_adapter, value_matrix, adapter_down, adapter_up):
    owner_count = lax.axis_size("adapter")
    req_count, decode_count, feature_count = hidden.shape
    adapter_number = adapter_down.shape[0]
    width_halved = adapter_down.shape[1]
    column_number = adapter_up.shape[2]
    capacity = 2 * req_count // owner_count
    sub_index = lax.axis_index("sub")
    owner_of = request_adapter // adapter_number
    local_id = request_adapter % adapter_number
    owner_hits = (owner_of[:, None] == jnp.arange(owner_count)[None, :]).astype(jnp.int32)
    earlier = jnp.cumsum(owner_hits, axis=0) - owner_hits
    slot_of = jnp.sum(earlier * owner_hits, axis=1)
    destination = owner_of * capacity + slot_of
    feature_half = lax.dynamic_slice_in_dim(hidden, sub_index * width_halved, width_halved, 2)
    outgoing = jnp.zeros((owner_count * capacity, decode_count, width_halved), hidden.dtype)
    outgoing = (
        outgoing.at[destination]
        .set(feature_half)
        .reshape(owner_count, capacity, decode_count, width_halved)
    )
    labels = jnp.full((owner_count * capacity,), -1, jnp.int32).at[destination].set(local_id)
    labels = labels.reshape(owner_count, capacity)
    rows_in = lax.all_to_all(outgoing, "adapter", split_axis=0, concat_axis=0, tiled=True)
    tag_ids = lax.all_to_all(labels, "adapter", split_axis=0, concat_axis=0, tiled=True)
    source_count, slot_count = tag_ids.shape
    place_total = source_count * slot_count
    flat_tags = jnp.maximum(tag_ids.reshape(place_total), 0)
    ordering = jnp.argsort(flat_tags, stable=True)
    restore = jnp.argsort(ordering, stable=True)
    ordered_rows = rows_in.reshape(place_total, decode_count, width_halved)[ordering]
    ordered_rows = ordered_rows.reshape(place_total * decode_count, width_halved)
    tag_hits = (flat_tags[:, None] == jnp.arange(adapter_number)[None, :]).astype(jnp.int32)
    group_lengths = jnp.sum(tag_hits, axis=0) * decode_count
    reduced_rows = lax.ragged_dot(
        ordered_rows, adapter_down, group_lengths, preferred_element_type=jnp.float32
    )
    reduced_rows = lax.psum(reduced_rows, "sub")
    update_rows = widen_rows(reduced_rows, adapter_up, group_lengths).reshape(
        place_total, decode_count, column_number
    )
    update_rows = update_rows[restore].reshape(
        source_count, slot_count, decode_count, column_number
    )
    returned = lax.all_to_all(update_rows, "adapter", split_axis=0, concat_axis=0, tiled=True)
    returned = returned.reshape(owner_count * capacity, decode_count, returned.shape[3])
    returned_rows = returned[destination]
    plain_rows = jnp.einsum("rsf,fc->rsc", hidden, value_matrix, preferred_element_type=jnp.float32)
    merged_output = plain_rows + adapter_scale * returned_rows
    summed = lax.psum(merged_output, "tensor")
    return summed.astype(jnp.bfloat16)


LAG = 2
TILE = 256
LANES = 128


def kernel(dims, hid_in, val_in, down_in, up_in, key, out, hid, val, w, up, acc, base, base_out, base_in,
           low_out, low_in, loc, zs, zr, ys, yr, xs, xr, bs, br, ls, lr):
    z_count, pairs, rank, feats = dims
    rows = acc.shape[0]
    half = pairs // 2
    x, y = lax.axis_index("tensor"), lax.axis_index("groups")
    z, s = lax.axis_index("adapter"), lax.axis_index("sub")
    quarter = up.shape[1] // 4
    mine_q = pl.ds(pl.multiple_of((2 * x + y) * quarter, quarter), quarter)
    other_q = pl.ds(pl.multiple_of((2 * x + 1 - y) * quarter, quarter), quarter)
    mine_h = pl.ds(pl.multiple_of(x * 2 * quarter, quarter), 2 * quarter)
    other_h = pl.ds(pl.multiple_of((1 - x) * 2 * quarter, quarter), 2 * quarter)
    cols = pl.ds(pl.multiple_of(s * feats, LANES), feats)
    to_y, to_x = {"groups": 1 - y}, {"tensor": 1 - x}
    peers = [{"tensor": 1 - x}, {"sub": 1 - s}, {"tensor": 1 - x, "sub": 1 - s}]

    def remote(src, dst, send, recv, dev):
        return pltpu.make_async_remote_copy(
            src_ref=src, dst_ref=dst, send_sem=send, recv_sem=recv,
            device_id=dev, device_id_type=pl.DeviceIdType.MESH)

    local_copies = [
        pltpu.make_async_copy(hid_in, hid, loc.at[0]),
        pltpu.make_async_copy(val_in, val, loc.at[1]),
        pltpu.make_async_copy(down_in, w.at[z], loc.at[2]),
        pltpu.make_async_copy(up_in, up.at[z], loc.at[3]),
    ]
    for copy in local_copies:
        copy.start()

    barrier = pltpu.get_barrier_semaphore()
    for dev in peers + [to_y]:
        pl.semaphore_signal(barrier, inc=1, device_id=dev, device_id_type=pl.DeviceIdType.MESH)

    @pl.when(z > 0)
    def _():
        pl.semaphore_signal(barrier, inc=1, device_id={"adapter": z - 1}, device_id_type=pl.DeviceIdType.MESH)

    @pl.when(z < z_count - 1)
    def _():
        pl.semaphore_signal(barrier, inc=1, device_id={"adapter": z + 1}, device_id_type=pl.DeviceIdType.MESH)

    ends = (z == 0).astype(jnp.int32) + (z == z_count - 1).astype(jnp.int32)
    pl.semaphore_wait(barrier, len(peers) + 3 - ends)

    def owner_of(d, t):
        return z - (1 - 2 * d) * t

    def target_of(d):
        return z + 1 - 2 * d

    def inside(k):
        return jnp.logical_and(k >= 0, k < z_count)

    def z_up(d, t, owner, src=None):
        ref = up.at[owner, mine_q]
        return remote(ref if src is None else src, ref, zs.at[d, t, half], zr.at[d, t, half],
                      {"adapter": target_of(d)})

    def z_down(d, t, owner, c, src=None):
        ref = w.at[owner, y * half + c]
        return remote(ref if src is None else src, ref, zs.at[d, t, c], zr.at[d, t, c],
                      {"adapter": target_of(d)})

    def y_up(d, t, owner, rows_at):
        ref = up.at[owner, rows_at]
        return remote(ref, ref, ys.at[d, t, half], yr.at[d, t, half], to_y)

    def y_down(d, t, owner, pair, c):
        ref = w.at[owner, pair]
        return remote(ref, ref, ys.at[d, t, c], yr.at[d, t, c], to_y)

    def x_up(d, t, owner, rows_at):
        ref = up.at[owner, rows_at]
        return remote(ref, ref, xs.at[d, t], xr.at[d, t], to_x)

    for d in range(2):
        @pl.when(inside(target_of(d)))
        def _(d=d):
            z_up(d, 1, z, up_in.at[mine_q]).start()
    for c in range(half):
        for d in range(2):
            @pl.when(inside(target_of(d)))
            def _(d=d, c=c):
                z_down(d, 1, z, c, down_in.at[y * half + c]).start()

    for copy in local_copies:
        copy.wait()

    base_copy = remote(base_out, base_in, bs, br, to_x)

    @pl.loop(0, rows // TILE)
    def _(r):
        at = pl.ds(pl.multiple_of(r * TILE, TILE), TILE)
        got = jnp.dot(hid[at, :], val[...], preferred_element_type=jnp.float32)
        base[at, :] = got
        base_out[at, :] = got.astype(jnp.bfloat16)
        acc[at, :] = jnp.zeros((TILE, LANES), jnp.float32)

    base_copy.start()

    def use(owner, pair):
        @pl.loop(0, rows // TILE)
        def _(r):
            at = pl.ds(pl.multiple_of(r * TILE, TILE), TILE)
            got = lax.dot_general(
                hid[at, cols], w[owner, pair], (((1,), (1,)), ((), ())), preferred_element_type=jnp.float32)
            acc[at, :] += jnp.where(key[at, :] == 2 * (owner * pairs + pair), got, 0.0)

    @pl.loop(0, pairs)
    def _(pair):
        use(z, pair)

    total = (z_count - 1) * half

    @pl.loop(0, total + LAG)
    def _(i):
        @pl.when(i < total)
        def _():
            t, c = i // half + 1, i % half

            @pl.loop(0, 2)
            def _(d):
                owner = owner_of(d, t)

                @pl.when(inside(owner))
                def _():
                    @pl.when(c == 0)
                    def _():
                        z_up(d, t, owner).wait_recv()

                        @pl.when(inside(target_of(d)))
                        def _():
                            z_up(d, t + 1, owner).start()

                        y_up(d, t, owner, mine_q).start()

                    z_down(d, t, owner, c).wait_recv()

                    @pl.when(inside(target_of(d)))
                    def _():
                        z_down(d, t + 1, owner, c).start()

                    y_down(d, t, owner, y * half + c, c).start()

            @pl.loop(0, 2)
            def _(d):
                owner = owner_of(d, t)

                @pl.when(inside(owner))
                def _():
                    use(owner, y * half + c)

        @pl.when(i >= LAG)
        def _():
            t, c = (i - LAG) // half + 1, (i - LAG) % half

            @pl.loop(0, 2)
            def _(d):
                owner = owner_of(d, t)

                @pl.when(inside(owner))
                def _():
                    @pl.when(c == 0)
                    def _():
                        y_up(d, t, owner, other_q).wait_recv()
                        x_up(d, t, owner, mine_h).start()

                    y_down(d, t, owner, (1 - y) * half + c, c).wait_recv()
                    use(owner, (1 - y) * half + c)

    mid = rows // 2
    lane = lax.broadcasted_iota(jnp.int32, (mid, LANES), 1)
    top = acc[:mid, :] + pltpu.roll(acc[:mid, :], rank, 1)
    bottom = acc[mid:, :] + pltpu.roll(acc[mid:, :], rank, 1)
    packed = jnp.where(lane < rank, top, bottom)
    low_out[...] = packed.astype(jnp.bfloat16)
    low_copies = [remote(low_out, low_in.at[n], ls.at[n], lr.at[n], dev) for n, dev in enumerate(peers)]
    for copy in low_copies:
        copy.start()

    @pl.loop(1, z_count)
    def _(t):
        @pl.loop(0, 2)
        def _(d):
            owner = owner_of(d, t)

            @pl.when(inside(owner))
            def _():
                x_up(d, t, owner, other_h).wait_recv()
                x_up(d, t, owner, mine_h).wait_send()
                y_up(d, t, owner, mine_q).wait_send()

                @pl.loop(0, half)
                def _(c):
                    y_down(d, t, owner, y * half + c, c).wait_send()

            before = owner_of(d, t - 1)

            @pl.when(jnp.logical_and(inside(before), inside(target_of(d))))
            def _():
                z_up(d, t, before).wait_send()

                @pl.loop(0, half)
                def _(c):
                    z_down(d, t, before, c).wait_send()

    base_copy.wait()
    for copy in low_copies:
        copy.wait()
    packed = packed + low_in[0].astype(jnp.float32) + low_in[1].astype(jnp.float32) + low_in[2].astype(jnp.float32)
    turned = pltpu.roll(packed, rank, 1)
    acc[:mid, :] = jnp.where(lane < rank, packed, turned)
    acc[mid:, :] = jnp.where(lane < rank, turned, packed)

    @pl.loop(0, rows // TILE)
    def _(r):
        at = pl.ds(pl.multiple_of(r * TILE, TILE), TILE)
        low, which = acc[at, :], key[at, :]
        delta = jnp.zeros((TILE, out.shape[1]), jnp.float32)
        for o in range(z_count):
            spread = jnp.concatenate(
                [jnp.where(which == 2 * (o * pairs + p), low, 0.0).astype(jnp.bfloat16) for p in range(pairs)], axis=1)
            delta += jnp.dot(spread, up[o], preferred_element_type=jnp.float32)
        sums = base[at, :] + base_in[at, :].astype(jnp.float32)
        out[at, :] = (sums + adapter_scale * delta).astype(jnp.bfloat16)


def gathered(hidden, request_adapter, value_matrix, adapter_down, adapter_up):
    z_count = lax.axis_size("adapter")
    reqs, steps, width = hidden.shape
    adapters, feats, rank = adapter_down.shape
    columns = adapter_up.shape[2]
    rows, pairs = reqs * steps, adapters // 2
    half = pairs // 2
    down = adapter_down.transpose(0, 2, 1).reshape(pairs, 2 * rank, feats)
    up = adapter_up.reshape(adapters * rank, columns)
    key = jnp.repeat(request_adapter, steps)[:, None] - (jnp.arange(2 * rank, dtype=jnp.int32) // rank)[None, :]
    bf, f32, dma = jnp.bfloat16, jnp.float32, pltpu.SemaphoreType.DMA
    anywhere = pl.BlockSpec(memory_space=pl.ANY)
    whole = pl.BlockSpec(memory_space=pltpu.VMEM)
    out = pl.pallas_call(
        functools.partial(kernel, (z_count, pairs, rank, feats)),
        out_shape=jax.ShapeDtypeStruct((rows, columns), bf),
        in_specs=[anywhere] * 4 + [whole],
        out_specs=whole,
        scratch_shapes=[
            pltpu.VMEM((rows, width), bf),
            pltpu.VMEM(value_matrix.shape, bf),
            pltpu.VMEM((z_count, pairs, 2 * rank, feats), bf),
            pltpu.VMEM((z_count, adapters * rank, columns), bf),
            pltpu.VMEM((rows, 2 * rank), f32),
            pltpu.VMEM((rows, columns), f32),
            pltpu.VMEM((rows, columns), bf),
            pltpu.VMEM((rows, columns), bf),
            pltpu.VMEM((rows // 2, 2 * rank), bf),
            pltpu.VMEM((3, rows // 2, 2 * rank), bf),
            dma((4,)),
            dma((2, z_count, half + 1)),
            dma((2, z_count, half + 1)),
            dma((2, z_count, half + 1)),
            dma((2, z_count, half + 1)),
            dma((2, z_count)),
            dma((2, z_count)),
            dma, dma,
            dma((3,)),
            dma((3,)),
        ],
        compiler_params=pltpu.CompilerParams(
            collective_id=0, has_side_effects=True, vmem_limit_bytes=60 * 2 ** 20),
        cost_estimate=pl.CostEstimate(flops=30 * 10 ** 9, bytes_accessed=20 * 10 ** 6, transcendentals=0),
    )(hidden.reshape(rows, width), value_matrix, down, up, key)
    return out.reshape(reqs, steps, columns)


def local(hidden, request_adapter, value_matrix, adapter_down, adapter_up):
    z_count = lax.axis_size("adapter")
    reqs, steps, width = hidden.shape
    maps = z_count * (adapter_down.size + adapter_up.size) * 2
    rest = (hidden.size + value_matrix.size) * 2 + reqs * steps * adapter_up.shape[2] * 10
    fits = maps + rest < 50 * 2 ** 20
    if fits and lax.axis_size("tensor") == 2 and lax.axis_size("groups") == 2 and lax.axis_size("sub") == 2:
        return gathered(hidden, request_adapter, value_matrix, adapter_down, adapter_up)
    return routed(hidden, request_adapter, value_matrix, adapter_down, adapter_up)


def solution(mesh):
    return jax.shard_map(
        local,
        mesh=mesh,
        in_specs=(
            P(("groups", "adapter"), None, "tensor"),
            P(("groups", "adapter")),
            P("tensor", "sub"),
            P("adapter", ("tensor", "sub"), None),
            P("adapter", None, "sub"),
        ),
        out_specs=P(("groups", "adapter"), None, "sub"),
        check_vma=False,
    )
```

```python
import functools

import jax
import jax.numpy as jnp
from jax import lax
from jax.experimental import pallas as pl
from jax.experimental.pallas import tpu as pltpu
from jax.sharding import PartitionSpec as P

adapter_scale = 0.5


def widen_rows(reduced_rows, up_table, group_lengths):
    high_part = reduced_rows.astype(jnp.bfloat16)
    low_part = (reduced_rows - high_part.astype(jnp.float32)).astype(jnp.bfloat16)
    first = lax.ragged_dot(high_part, up_table, group_lengths, preferred_element_type=jnp.float32)
    second = lax.ragged_dot(low_part, up_table, group_lengths, preferred_element_type=jnp.float32)
    return first + second


def routed(hidden, request_adapter, value_matrix, adapter_down, adapter_up):
    owner_count = lax.axis_size("adapter")
    req_count, decode_count, feature_count = hidden.shape
    adapter_number = adapter_down.shape[0]
    width_halved = adapter_down.shape[1]
    column_number = adapter_up.shape[2]
    capacity = 2 * req_count // owner_count
    sub_index = lax.axis_index("sub")
    owner_of = request_adapter // adapter_number
    local_id = request_adapter % adapter_number
    owner_hits = (owner_of[:, None] == jnp.arange(owner_count)[None, :]).astype(jnp.int32)
    earlier = jnp.cumsum(owner_hits, axis=0) - owner_hits
    slot_of = jnp.sum(earlier * owner_hits, axis=1)
    destination = owner_of * capacity + slot_of
    feature_half = lax.dynamic_slice_in_dim(hidden, sub_index * width_halved, width_halved, 2)
    outgoing = jnp.zeros((owner_count * capacity, decode_count, width_halved), hidden.dtype)
    outgoing = (
        outgoing.at[destination]
        .set(feature_half)
        .reshape(owner_count, capacity, decode_count, width_halved)
    )
    labels = jnp.full((owner_count * capacity,), -1, jnp.int32).at[destination].set(local_id)
    labels = labels.reshape(owner_count, capacity)
    rows_in = lax.all_to_all(outgoing, "adapter", split_axis=0, concat_axis=0, tiled=True)
    tag_ids = lax.all_to_all(labels, "adapter", split_axis=0, concat_axis=0, tiled=True)
    source_count, slot_count = tag_ids.shape
    place_total = source_count * slot_count
    flat_tags = jnp.maximum(tag_ids.reshape(place_total), 0)
    ordering = jnp.argsort(flat_tags, stable=True)
    restore = jnp.argsort(ordering, stable=True)
    ordered_rows = rows_in.reshape(place_total, decode_count, width_halved)[ordering]
    ordered_rows = ordered_rows.reshape(place_total * decode_count, width_halved)
    tag_hits = (flat_tags[:, None] == jnp.arange(adapter_number)[None, :]).astype(jnp.int32)
    group_lengths = jnp.sum(tag_hits, axis=0) * decode_count
    reduced_rows = lax.ragged_dot(
        ordered_rows, adapter_down, group_lengths, preferred_element_type=jnp.float32
    )
    reduced_rows = lax.psum(reduced_rows, "sub")
    update_rows = widen_rows(reduced_rows, adapter_up, group_lengths).reshape(
        place_total, decode_count, column_number
    )
    update_rows = update_rows[restore].reshape(
        source_count, slot_count, decode_count, column_number
    )
    returned = lax.all_to_all(update_rows, "adapter", split_axis=0, concat_axis=0, tiled=True)
    returned = returned.reshape(owner_count * capacity, decode_count, returned.shape[3])
    returned_rows = returned[destination]
    plain_rows = jnp.einsum("rsf,fc->rsc", hidden, value_matrix, preferred_element_type=jnp.float32)
    merged_output = plain_rows + adapter_scale * returned_rows
    summed = lax.psum(merged_output, "tensor")
    return summed.astype(jnp.bfloat16)


TILE = 256
LANES = 128


def kernel(dims, hid_in, val_in, down_in, up_in, key, out, hid3, hid, hidy3, hidy, keyy, val, w, up, acc, accy, base,
           base_out, base_in, low_out, low_in, loc, zs, zr, us, ur, xs, xr, hs, hr, bs, br, ls, lr):
    z_count, pairs, rank, feats = dims
    rows = acc.shape[0]
    steps = hid3.shape[1]
    half = pairs // 2
    tiles, step_rows = rows // TILE, TILE // steps
    x, y = lax.axis_index("tensor"), lax.axis_index("groups")
    z, s = lax.axis_index("adapter"), lax.axis_index("sub")
    quarter = up.shape[1] // 4
    mine_q = pl.ds(pl.multiple_of((2 * x + y) * quarter, quarter), quarter)
    other_q = pl.ds(pl.multiple_of((2 * x + 1 - y) * quarter, quarter), quarter)
    mine_h = pl.ds(pl.multiple_of(x * 2 * quarter, quarter), 2 * quarter)
    other_h = pl.ds(pl.multiple_of((1 - x) * 2 * quarter, quarter), 2 * quarter)
    cols = pl.ds(pl.multiple_of(s * feats, LANES), feats)
    my_half = pl.ds(y * half, half)
    to_y, to_x = {"groups": 1 - y}, {"tensor": 1 - x}
    peers = [{"tensor": 1 - x}, {"sub": 1 - s}, {"tensor": 1 - x, "sub": 1 - s},
             {"groups": 1 - y}, {"groups": 1 - y, "tensor": 1 - x}, {"groups": 1 - y, "sub": 1 - s},
             {"groups": 1 - y, "tensor": 1 - x, "sub": 1 - s}]

    def remote(src, dst, send, recv, dev):
        return pltpu.make_async_remote_copy(
            src_ref=src, dst_ref=dst, send_sem=send, recv_sem=recv,
            device_id=dev, device_id_type=pl.DeviceIdType.MESH)

    def signal(dev, barrier):
        pl.semaphore_signal(barrier, inc=1, device_id=dev, device_id_type=pl.DeviceIdType.MESH)

    local_copies = [
        pltpu.make_async_copy(hid_in, hid3, loc.at[0]),
        pltpu.make_async_copy(val_in, val, loc.at[1]),
        pltpu.make_async_copy(down_in.at[my_half], w.at[z], loc.at[2]),
        pltpu.make_async_copy(up_in, up.at[z], loc.at[3]),
    ]
    for copy in local_copies:
        copy.start()

    barrier = pltpu.get_barrier_semaphore()
    for dev in peers:
        signal(dev, barrier)

    @pl.when(z > 0)
    def _():
        signal({"adapter": z - 1}, barrier)

    @pl.when(z < z_count - 1)
    def _():
        signal({"adapter": z + 1}, barrier)

    ends = (z == 0).astype(jnp.int32) + (z == z_count - 1).astype(jnp.int32)
    pl.semaphore_wait(barrier, len(peers) + 2 - ends)

    def owner_of(d, t):
        return z - (1 - 2 * d) * t

    def target_of(d):
        return z + 1 - 2 * d

    def inside(k):
        return jnp.logical_and(k >= 0, k < z_count)

    def z_up(d, t, owner, src=None):
        ref = up.at[owner, mine_q]
        return remote(ref if src is None else src, ref, zs.at[d, t, half], zr.at[d, t, half],
                      {"adapter": target_of(d)})

    def z_down(d, t, owner, c, src=None):
        ref = w.at[owner, c]
        return remote(ref if src is None else src, ref, zs.at[d, t, c], zr.at[d, t, c],
                      {"adapter": target_of(d)})

    def y_up(d, t, owner, rows_at):
        ref = up.at[owner, rows_at]
        return remote(ref, ref, us.at[d, t], ur.at[d, t], to_y)

    def x_up(d, t, owner, rows_at):
        ref = up.at[owner, rows_at]
        return remote(ref, ref, xs.at[d, t], xr.at[d, t], to_x)

    key_copy = remote(key, keyy, hs.at[tiles], hr.at[tiles], to_y)

    def hidden_copy(r):
        at = pl.ds(r * step_rows, step_rows)
        return remote(hid_in.at[at, :, cols], hidy3.at[at], hs.at[r], hr.at[r], to_y)

    for d in range(2):
        @pl.when(inside(target_of(d)))
        def _(d=d):
            z_up(d, 1, z, up_in.at[mine_q]).start()
    for c in range(half):
        for d in range(2):
            @pl.when(inside(target_of(d)))
            def _(d=d, c=c):
                z_down(d, 1, z, c, down_in.at[y * half + c]).start()
    key_copy.start()
    for r in range(tiles):
        hidden_copy(r).start()

    for copy in local_copies:
        copy.wait()

    base_copy = remote(base_out, base_in, bs, br, to_x)

    def tile_at(r):
        return pl.ds(pl.multiple_of(r * TILE, TILE), TILE)

    @pl.loop(0, tiles)
    def _(r):
        at = tile_at(r)
        part = hid3[pl.ds(r * step_rows, step_rows)].reshape(TILE, hid.shape[1])
        hid[at, :] = part
        got = jnp.dot(part, val[...], preferred_element_type=jnp.float32)
        base[at, :] = got
        base_out[at, :] = got.astype(jnp.bfloat16)
        acc[at, :] = jnp.zeros((TILE, LANES), jnp.float32)
        accy[at, :] = jnp.zeros((TILE, LANES), jnp.float32)

    base_copy.start()

    def add(part, which, total, at, owner):
        maps = w[owner].reshape(half * LANES, feats)
        got = lax.dot_general(part, maps, (((1,), (1,)), ((), ())), preferred_element_type=jnp.float32)
        first = 2 * (owner * pairs + y * half)
        ids = which[at, :] - first
        more = total[at, :]
        for p in range(half):
            more += jnp.where(ids == 2 * p, got[:, p * LANES:(p + 1) * LANES], 0.0)
        total[at, :] = more

    def use(owner):
        @pl.loop(0, tiles)
        def _(r):
            at = tile_at(r)
            add(hid[at, cols], key, acc, at, owner)

    def use_other(owner, r):
        at = tile_at(r)
        add(hidy[at, :], keyy, accy, at, owner)

    use(z)

    @pl.loop(1, z_count)
    def _(t):
        last = t == z_count - 1

        @pl.loop(0, half)
        def _(c):
            @pl.loop(0, 2)
            def _(d):
                owner = owner_of(d, t)

                @pl.when(inside(owner))
                def _():
                    @pl.when(c == 0)
                    def _():
                        z_up(d, t, owner).wait_recv()

                        @pl.when(inside(target_of(d)))
                        def _():
                            z_up(d, t + 1, owner).start()

                        y_up(d, t, owner, mine_q).start()

                    z_down(d, t, owner, c).wait_recv()

                    @pl.when(inside(target_of(d)))
                    def _():
                        z_down(d, t + 1, owner, c).start()

            @pl.when(jnp.logical_and(last, c == 1))
            def _():
                @pl.loop(1, z_count)
                def _(k):
                    @pl.loop(0, 2)
                    def _(d):
                        owner = owner_of(d, k)

                        @pl.when(inside(owner))
                        def _():
                            y_up(d, k, owner, other_q).wait_recv()
                            x_up(d, k, owner, mine_h).start()

        @pl.loop(0, 2)
        def _(d):
            owner = owner_of(d, t)

            @pl.when(inside(owner))
            def _():
                use(owner)

        @pl.when(t == z_count - 2)
        def _():
            key_copy.wait_recv()

            @pl.loop(0, tiles)
            def _(r):
                hidden_copy(r).wait_recv()
                hidy[tile_at(r), :] = hidy3[pl.ds(r * step_rows, step_rows)].reshape(TILE, feats)

                @pl.loop(0, z_count)
                def _(owner):
                    @pl.when(jnp.logical_and(owner - z < z_count - 1, z - owner < z_count - 1))
                    def _():
                        use_other(owner, r)

        @pl.when(last)
        def _():
            @pl.loop(0, 2)
            def _(d):
                owner = owner_of(d, t)

                @pl.when(inside(owner))
                def _():
                    @pl.loop(0, tiles)
                    def _(r):
                        use_other(owner, r)

    mid = rows // 2
    lane = lax.broadcasted_iota(jnp.int32, (mid, LANES), 1)

    def pack(total):
        top = total[:mid, :] + pltpu.roll(total[:mid, :], rank, 1)
        bottom = total[mid:, :] + pltpu.roll(total[mid:, :], rank, 1)
        return jnp.where(lane < rank, top, bottom)

    low_out[1] = pack(accy).astype(jnp.bfloat16)
    low_out[0] = pack(acc).astype(jnp.bfloat16)
    low_copies = [
        remote(low_out.at[0 if n < 3 else 1], low_in.at[n], ls.at[n], lr.at[n], dev) for n, dev in enumerate(peers)]
    for copy in low_copies:
        copy.start()

    @pl.loop(1, z_count)
    def _(t):
        @pl.loop(0, 2)
        def _(d):
            owner = owner_of(d, t)

            @pl.when(inside(owner))
            def _():
                x_up(d, t, owner, other_h).wait_recv()
                x_up(d, t, owner, mine_h).wait_send()
                y_up(d, t, owner, mine_q).wait_send()

            before = owner_of(d, t - 1)

            @pl.when(jnp.logical_and(inside(before), inside(target_of(d))))
            def _():
                z_up(d, t, before).wait_send()

                @pl.loop(0, half)
                def _(c):
                    z_down(d, t, before, c).wait_send()

    key_copy.wait_send()
    for r in range(tiles):
        hidden_copy(r).wait_send()
    base_copy.wait()
    for copy in low_copies:
        copy.wait()
    packed = pack(acc)
    for n in range(len(peers)):
        packed += low_in[n].astype(jnp.float32)
    turned = pltpu.roll(packed, rank, 1)
    acc[:mid, :] = jnp.where(lane < rank, packed, turned)
    acc[mid:, :] = jnp.where(lane < rank, turned, packed)

    @pl.loop(0, tiles)
    def _(r):
        at = tile_at(r)
        low, which = acc[at, :], key[at, :]
        delta = jnp.zeros((TILE, base.shape[1]), jnp.float32)
        for o in range(z_count):
            spread = jnp.concatenate(
                [jnp.where(which == 2 * (o * pairs + p), low, 0.0).astype(jnp.bfloat16) for p in range(pairs)], axis=1)
            delta += jnp.dot(spread, up[o], preferred_element_type=jnp.float32)
        sums = base[at, :] + base_in[at, :].astype(jnp.float32)
        result = (sums + adapter_scale * delta).astype(jnp.bfloat16)
        out[pl.ds(r * step_rows, step_rows)] = result.reshape(step_rows, steps, base.shape[1])


def gathered(hidden, request_adapter, value_matrix, adapter_down, adapter_up):
    z_count = lax.axis_size("adapter")
    reqs, steps, width = hidden.shape
    adapters, feats, rank = adapter_down.shape
    columns = adapter_up.shape[2]
    rows, pairs = reqs * steps, adapters // 2
    half = pairs // 2
    down = adapter_down.transpose(0, 2, 1).reshape(pairs, 2 * rank, feats)
    up = adapter_up.reshape(adapters * rank, columns)
    key = jnp.repeat(request_adapter, steps)[:, None] - (jnp.arange(2 * rank, dtype=jnp.int32) // rank)[None, :]
    bf, f32, dma = jnp.bfloat16, jnp.float32, pltpu.SemaphoreType.DMA
    anywhere = pl.BlockSpec(memory_space=pl.ANY)
    whole = pl.BlockSpec(memory_space=pltpu.VMEM)
    return pl.pallas_call(
        functools.partial(kernel, (z_count, pairs, rank, feats)),
        out_shape=jax.ShapeDtypeStruct((reqs, steps, columns), bf),
        in_specs=[anywhere] * 4 + [whole],
        out_specs=whole,
        scratch_shapes=[
            pltpu.VMEM(hidden.shape, bf),
            pltpu.VMEM((rows, width), bf),
            pltpu.VMEM((reqs, steps, feats), bf),
            pltpu.VMEM((rows, feats), bf),
            pltpu.VMEM((rows, 2 * rank), jnp.int32),
            pltpu.VMEM(value_matrix.shape, bf),
            pltpu.VMEM((z_count, half, 2 * rank, feats), bf),
            pltpu.VMEM((z_count, adapters * rank, columns), bf),
            pltpu.VMEM((rows, 2 * rank), f32),
            pltpu.VMEM((rows, 2 * rank), f32),
            pltpu.VMEM((rows, columns), f32),
            pltpu.VMEM((rows, columns), bf),
            pltpu.VMEM((rows, columns), bf),
            pltpu.VMEM((2, rows // 2, 2 * rank), bf),
            pltpu.VMEM((7, rows // 2, 2 * rank), bf),
            dma((4,)),
            dma((2, z_count, half + 1)),
            dma((2, z_count, half + 1)),
            dma((2, z_count)),
            dma((2, z_count)),
            dma((2, z_count)),
            dma((2, z_count)),
            dma((rows // TILE + 1,)),
            dma((rows // TILE + 1,)),
            dma, dma,
            dma((7,)),
            dma((7,)),
        ],
        compiler_params=pltpu.CompilerParams(
            collective_id=0, has_side_effects=True, vmem_limit_bytes=60 * 2 ** 20),
        cost_estimate=pl.CostEstimate(flops=30 * 10 ** 9, bytes_accessed=20 * 10 ** 6, transcendentals=0),
    )(hidden, value_matrix, down, up, key)


def local(hidden, request_adapter, value_matrix, adapter_down, adapter_up):
    z_count = lax.axis_size("adapter")
    reqs, steps, width = hidden.shape
    maps = z_count * (adapter_down.size + adapter_up.size) * 2
    rest = (hidden.size + value_matrix.size) * 2 + reqs * steps * adapter_up.shape[2] * 10
    fits = maps + rest < 50 * 2 ** 20
    if fits and lax.axis_size("tensor") == 2 and lax.axis_size("groups") == 2 and lax.axis_size("sub") == 2:
        return gathered(hidden, request_adapter, value_matrix, adapter_down, adapter_up)
    return routed(hidden, request_adapter, value_matrix, adapter_down, adapter_up)


def solution(mesh):
    return jax.shard_map(
        local,
        mesh=mesh,
        in_specs=(
            P(("groups", "adapter"), None, "tensor"),
            P(("groups", "adapter")),
            P("tensor", "sub"),
            P("adapter", ("tensor", "sub"), None),
            P("adapter", None, "sub"),
        ),
        out_specs=P(("groups", "adapter"), None, "sub"),
        check_vma=False,
    )
```

```python
import functools

import jax
import jax.numpy as jnp
from jax import lax
from jax.experimental import pallas as pl
from jax.experimental.pallas import tpu as pltpu
from jax.sharding import PartitionSpec as P

adapter_scale = 0.5


def widen_rows(reduced_rows, up_table, group_lengths):
    high_part = reduced_rows.astype(jnp.bfloat16)
    low_part = (reduced_rows - high_part.astype(jnp.float32)).astype(jnp.bfloat16)
    first = lax.ragged_dot(high_part, up_table, group_lengths, preferred_element_type=jnp.float32)
    second = lax.ragged_dot(low_part, up_table, group_lengths, preferred_element_type=jnp.float32)
    return first + second


def routed(hidden, request_adapter, value_matrix, adapter_down, adapter_up):
    owner_count = lax.axis_size("adapter")
    req_count, decode_count, feature_count = hidden.shape
    adapter_number = adapter_down.shape[0]
    width_halved = adapter_down.shape[1]
    column_number = adapter_up.shape[2]
    capacity = 2 * req_count // owner_count
    sub_index = lax.axis_index("sub")
    owner_of = request_adapter // adapter_number
    local_id = request_adapter % adapter_number
    owner_hits = (owner_of[:, None] == jnp.arange(owner_count)[None, :]).astype(jnp.int32)
    earlier = jnp.cumsum(owner_hits, axis=0) - owner_hits
    slot_of = jnp.sum(earlier * owner_hits, axis=1)
    destination = owner_of * capacity + slot_of
    feature_half = lax.dynamic_slice_in_dim(hidden, sub_index * width_halved, width_halved, 2)
    outgoing = jnp.zeros((owner_count * capacity, decode_count, width_halved), hidden.dtype)
    outgoing = (
        outgoing.at[destination]
        .set(feature_half)
        .reshape(owner_count, capacity, decode_count, width_halved)
    )
    labels = jnp.full((owner_count * capacity,), -1, jnp.int32).at[destination].set(local_id)
    labels = labels.reshape(owner_count, capacity)
    rows_in = lax.all_to_all(outgoing, "adapter", split_axis=0, concat_axis=0, tiled=True)
    tag_ids = lax.all_to_all(labels, "adapter", split_axis=0, concat_axis=0, tiled=True)
    source_count, slot_count = tag_ids.shape
    place_total = source_count * slot_count
    flat_tags = jnp.maximum(tag_ids.reshape(place_total), 0)
    ordering = jnp.argsort(flat_tags, stable=True)
    restore = jnp.argsort(ordering, stable=True)
    ordered_rows = rows_in.reshape(place_total, decode_count, width_halved)[ordering]
    ordered_rows = ordered_rows.reshape(place_total * decode_count, width_halved)
    tag_hits = (flat_tags[:, None] == jnp.arange(adapter_number)[None, :]).astype(jnp.int32)
    group_lengths = jnp.sum(tag_hits, axis=0) * decode_count
    reduced_rows = lax.ragged_dot(
        ordered_rows, adapter_down, group_lengths, preferred_element_type=jnp.float32
    )
    reduced_rows = lax.psum(reduced_rows, "sub")
    update_rows = widen_rows(reduced_rows, adapter_up, group_lengths).reshape(
        place_total, decode_count, column_number
    )
    update_rows = update_rows[restore].reshape(
        source_count, slot_count, decode_count, column_number
    )
    returned = lax.all_to_all(update_rows, "adapter", split_axis=0, concat_axis=0, tiled=True)
    returned = returned.reshape(owner_count * capacity, decode_count, returned.shape[3])
    returned_rows = returned[destination]
    plain_rows = jnp.einsum("rsf,fc->rsc", hidden, value_matrix, preferred_element_type=jnp.float32)
    merged_output = plain_rows + adapter_scale * returned_rows
    summed = lax.psum(merged_output, "tensor")
    return summed.astype(jnp.bfloat16)


TILE = 256
LANES = 128


def kernel(dims, hid_in, val_in, down_in, up_in, key, out, hid3, hid, hidy3, hidy, keyy, val, w, up, acc, accy, base,
           base_out, base_in, low_out, low_in, wown, hidr3, keyr, accr, own, back_out, back_in, rs, rr, loc, zs, zr, us, ur, xs, xr, hs, hr, bs, br, ls, lr):
    z_count, pairs, rank, feats = dims
    rows = acc.shape[0]
    steps = hid3.shape[1]
    half = pairs // 2
    tiles, step_rows = rows // TILE, TILE // steps
    x, y = lax.axis_index("tensor"), lax.axis_index("groups")
    z, s = lax.axis_index("adapter"), lax.axis_index("sub")
    quarter = up.shape[1] // 4
    mine_q = pl.ds(pl.multiple_of((2 * x + y) * quarter, quarter), quarter)
    other_q = pl.ds(pl.multiple_of((2 * x + 1 - y) * quarter, quarter), quarter)
    mine_h = pl.ds(pl.multiple_of(x * 2 * quarter, quarter), 2 * quarter)
    other_h = pl.ds(pl.multiple_of((1 - x) * 2 * quarter, quarter), 2 * quarter)
    cols = pl.ds(pl.multiple_of(s * feats, LANES), feats)
    my_half = pl.ds(y * half, half)
    to_y, to_x = {"groups": 1 - y}, {"tensor": 1 - x}
    peers = [{"tensor": 1 - x}, {"sub": 1 - s}, {"tensor": 1 - x, "sub": 1 - s},
             {"groups": 1 - y}, {"groups": 1 - y, "tensor": 1 - x}, {"groups": 1 - y, "sub": 1 - s},
             {"groups": 1 - y, "tensor": 1 - x, "sub": 1 - s}]

    def remote(src, dst, send, recv, dev):
        return pltpu.make_async_remote_copy(
            src_ref=src, dst_ref=dst, send_sem=send, recv_sem=recv,
            device_id=dev, device_id_type=pl.DeviceIdType.MESH)

    def signal(dev, barrier):
        pl.semaphore_signal(barrier, inc=1, device_id=dev, device_id_type=pl.DeviceIdType.MESH)

    local_copies = [
        pltpu.make_async_copy(hid_in, hid3, loc.at[0]),
        pltpu.make_async_copy(val_in, val, loc.at[1]),
        pltpu.make_async_copy(down_in.at[my_half], w.at[z], loc.at[2]),
        pltpu.make_async_copy(up_in, up.at[z], loc.at[3]),
        pltpu.make_async_copy(down_in.at[:, :, pl.ds(0, feats // 2)], wown, loc.at[4]),
    ]
    for copy in local_copies:
        copy.start()

    barrier = pltpu.get_barrier_semaphore()
    for dev in peers:
        signal(dev, barrier)

    @pl.when(z > 0)
    def _():
        signal({"adapter": z - 1}, barrier)

    @pl.when(z < z_count - 1)
    def _():
        signal({"adapter": z + 1}, barrier)

    ends = (z == 0).astype(jnp.int32) + (z == z_count - 1).astype(jnp.int32)
    pl.semaphore_wait(barrier, len(peers) + 2 - ends)

    def owner_of(d, t):
        return z - (1 - 2 * d) * t

    def target_of(d):
        return z + 1 - 2 * d

    def inside(k):
        return jnp.logical_and(k >= 0, k < z_count)

    def z_up(d, t, owner, src=None):
        ref = up.at[owner, mine_q]
        return remote(ref if src is None else src, ref, zs.at[d, t, half], zr.at[d, t, half],
                      {"adapter": target_of(d)})

    def z_down(d, t, owner, c, src=None):
        ref = w.at[owner, c]
        return remote(ref if src is None else src, ref, zs.at[d, t, c], zr.at[d, t, c],
                      {"adapter": target_of(d)})

    fh = feats // 2

    def end(k):
        return jnp.logical_or(k == 0, k == z_count - 1)

    server = jnp.logical_or(z == 1, z == z_count - 2)
    partner = jnp.where(z == 0, 1, jnp.where(z == z_count - 1, z_count - 2, jnp.where(z == 1, 0, z_count - 1)))

    def z_part(d, owner, c):
        at = pl.ds(fh, fh)
        return remote(down_in.at[y * half + c, :, at], w.at[owner, c, :, at], zs.at[d, 1, c], zr.at[d, 1, c],
                      {"adapter": target_of(d)})

    first_cols = pl.ds(pl.multiple_of(s * feats, LANES), fh)
    route = [
        remote(hid_in.at[:, :, first_cols], hidr3, rs.at[0], rr.at[0], {"adapter": partner}),
        remote(key, keyr, rs.at[1], rr.at[1], {"adapter": partner}),
    ]
    route_back = remote(back_out, back_in, rs.at[2], rr.at[2], {"adapter": partner})

    def y_up(d, t, owner, rows_at):
        ref = up.at[owner, rows_at]
        return remote(ref, ref, us.at[d, t], ur.at[d, t], to_y)

    def x_up(d, t, owner, rows_at):
        ref = up.at[owner, rows_at]
        return remote(ref, ref, xs.at[d, t], xr.at[d, t], to_x)

    key_copy = remote(key, keyy, hs.at[tiles], hr.at[tiles], to_y)

    def hidden_copy(r):
        at = pl.ds(r * step_rows, step_rows)
        return remote(hid_in.at[at, :, cols], hidy3.at[at], hs.at[r], hr.at[r], to_y)

    for d in range(2):
        @pl.when(inside(target_of(d)))
        def _(d=d):
            z_up(d, 1, z, up_in.at[mine_q]).start()
    for c in range(half):
        for d in range(2):
            @pl.when(jnp.logical_and(inside(target_of(d)), jnp.logical_not(end(target_of(d)))))
            def _(d=d, c=c):
                z_down(d, 1, z, c, down_in.at[y * half + c]).start()

            @pl.when(end(target_of(d)))
            def _(d=d, c=c):
                z_part(d, z, c).start()

    @pl.when(end(z))
    def _():
        for copy in route:
            copy.start()

    key_copy.start()
    for r in range(tiles):
        hidden_copy(r).start()

    for copy in local_copies:
        copy.wait()

    base_copy = remote(base_out, base_in, bs, br, to_x)

    def tile_at(r):
        return pl.ds(pl.multiple_of(r * TILE, TILE), TILE)

    @pl.loop(0, tiles)
    def _(r):
        at = tile_at(r)
        part = hid3[pl.ds(r * step_rows, step_rows)].reshape(TILE, hid.shape[1])
        hid[at, :] = part
        got = jnp.dot(part, val[...], preferred_element_type=jnp.float32)
        base[at, :] = got
        base_out[at, :] = got.astype(jnp.bfloat16)
        acc[at, :] = jnp.zeros((TILE, LANES), jnp.float32)
        accy[at, :] = jnp.zeros((TILE, LANES), jnp.float32)
        accr[at, :] = jnp.zeros((TILE, LANES), jnp.float32)

    base_copy.start()

    def add(part, maps, which, total, at, first):
        got = lax.dot_general(part, maps, (((1,), (1,)), ((), ())), preferred_element_type=jnp.float32)
        ids = which[at, :] - 2 * first
        more = total[at, :]
        for p in range(half):
            more += jnp.where(ids == 2 * p, got[:, p * LANES:(p + 1) * LANES], 0.0)
        total[at, :] = more

    late_cols = pl.ds(pl.multiple_of(s * feats + fh, LANES), fh)

    def meet(rows_ref, all_cols, cut_cols, which, total, owner, r):
        at = tile_at(r)
        first = owner * pairs + y * half
        cut = jnp.logical_and(end(z), owner == partner)

        @pl.when(cut)
        def _():
            maps = w[owner, :, :, fh:].reshape(half * LANES, fh)
            add(rows_ref[at, cut_cols], maps, which, total, at, first)

        @pl.when(jnp.logical_not(cut))
        def _():
            maps = w[owner].reshape(half * LANES, feats)
            add(rows_ref[at, all_cols], maps, which, total, at, first)

    def use(owner):
        @pl.loop(0, tiles)
        def _(r):
            meet(hid, cols, late_cols, key, acc, owner, r)

    def use_other(owner, r):
        meet(hidy, pl.ds(0, feats), pl.ds(fh, fh), keyy, accy, owner, r)

    use(z)

    @pl.loop(1, z_count)
    def _(t):
        last = t == z_count - 1

        @pl.loop(0, half)
        def _(c):
            @pl.loop(0, 2)
            def _(d):
                owner = owner_of(d, t)

                @pl.when(inside(owner))
                def _():
                    @pl.when(c == 0)
                    def _():
                        z_up(d, t, owner).wait_recv()

                        @pl.when(inside(target_of(d)))
                        def _():
                            z_up(d, t + 1, owner).start()

                        y_up(d, t, owner, mine_q).start()

                    cut = jnp.logical_and(t == 1, end(z))

                    @pl.when(cut)
                    def _():
                        z_part(d, owner, c).wait_recv()

                    @pl.when(jnp.logical_not(cut))
                    def _():
                        z_down(d, t, owner, c).wait_recv()

                    @pl.when(inside(target_of(d)))
                    def _():
                        z_down(d, t + 1, owner, c).start()

            @pl.when(jnp.logical_and(last, c == 1))
            def _():
                @pl.loop(1, z_count)
                def _(k):
                    @pl.loop(0, 2)
                    def _(d):
                        owner = owner_of(d, k)

                        @pl.when(inside(owner))
                        def _():
                            y_up(d, k, owner, other_q).wait_recv()
                            x_up(d, k, owner, mine_h).start()

        @pl.loop(0, 2)
        def _(d):
            owner = owner_of(d, t)

            @pl.when(inside(owner))
            def _():
                use(owner)

        @pl.when(t == z_count - 2)
        def _():
            key_copy.wait_recv()

            @pl.loop(0, tiles)
            def _(r):
                hidden_copy(r).wait_recv()
                hidy[tile_at(r), :] = hidy3[pl.ds(r * step_rows, step_rows)].reshape(TILE, feats)

                @pl.loop(0, z_count)
                def _(owner):
                    @pl.when(jnp.logical_and(owner - z < z_count - 1, z - owner < z_count - 1))
                    def _():
                        use_other(owner, r)

        @pl.when(last)
        def _():
            @pl.loop(0, 2)
            def _(d):
                owner = owner_of(d, t)

                @pl.when(inside(owner))
                def _():
                    @pl.loop(0, tiles)
                    def _(r):
                        use_other(owner, r)

    mid = rows // 2
    lane = lax.broadcasted_iota(jnp.int32, (mid, LANES), 1)

    def pack(total):
        top = total[:mid, :] + pltpu.roll(total[:mid, :], rank, 1)
        bottom = total[mid:, :] + pltpu.roll(total[mid:, :], rank, 1)
        return jnp.where(lane < rank, top, bottom)

    low_out[1] = pack(accy).astype(jnp.bfloat16)
    own[...] = pack(acc)

    @pl.when(server)
    def _():
        for copy in route:
            copy.wait_recv()

        @pl.loop(0, tiles)
        def _(r):
            part = hidr3[pl.ds(r * step_rows, step_rows)].reshape(TILE, fh)
            for h in range(2):
                maps = wown[h * half:(h + 1) * half].reshape(half * LANES, fh)
                add(part, maps, keyr, accr, tile_at(r), z * pairs + h * half)

        back_out[...] = pack(accr).astype(jnp.bfloat16)
        route_back.start()

    @pl.when(end(z))
    def _():
        route_back.wait_recv()
        own[...] += back_in[...].astype(jnp.float32)

    low_out[0] = own[...].astype(jnp.bfloat16)
    low_copies = [
        remote(low_out.at[0 if n < 3 else 1], low_in.at[n], ls.at[n], lr.at[n], dev) for n, dev in enumerate(peers)]
    for copy in low_copies:
        copy.start()

    @pl.loop(1, z_count)
    def _(t):
        @pl.loop(0, 2)
        def _(d):
            owner = owner_of(d, t)

            @pl.when(inside(owner))
            def _():
                x_up(d, t, owner, other_h).wait_recv()
                x_up(d, t, owner, mine_h).wait_send()
                y_up(d, t, owner, mine_q).wait_send()

            before = owner_of(d, t - 1)

            @pl.when(jnp.logical_and(inside(before), inside(target_of(d))))
            def _():
                z_up(d, t, before).wait_send()

                @pl.loop(0, half)
                def _(c):
                    cut = jnp.logical_and(t == 1, end(target_of(d)))

                    @pl.when(cut)
                    def _():
                        z_part(d, before, c).wait_send()

                    @pl.when(jnp.logical_not(cut))
                    def _():
                        z_down(d, t, before, c).wait_send()

    @pl.when(server)
    def _():
        route_back.wait_send()

    @pl.when(end(z))
    def _():
        for copy in route:
            copy.wait_send()

    key_copy.wait_send()
    for r in range(tiles):
        hidden_copy(r).wait_send()
    base_copy.wait()
    for copy in low_copies:
        copy.wait()
    packed = own[...]
    for n in range(len(peers)):
        packed += low_in[n].astype(jnp.float32)
    turned = pltpu.roll(packed, rank, 1)
    acc[:mid, :] = jnp.where(lane < rank, packed, turned)
    acc[mid:, :] = jnp.where(lane < rank, turned, packed)

    @pl.loop(0, tiles)
    def _(r):
        at = tile_at(r)
        low, which = acc[at, :], key[at, :]
        delta = jnp.zeros((TILE, base.shape[1]), jnp.float32)
        for o in range(z_count):
            spread = jnp.concatenate(
                [jnp.where(which == 2 * (o * pairs + p), low, 0.0).astype(jnp.bfloat16) for p in range(pairs)], axis=1)
            delta += jnp.dot(spread, up[o], preferred_element_type=jnp.float32)
        sums = base[at, :] + base_in[at, :].astype(jnp.float32)
        result = (sums + adapter_scale * delta).astype(jnp.bfloat16)
        out[pl.ds(r * step_rows, step_rows)] = result.reshape(step_rows, steps, base.shape[1])


def gathered(hidden, request_adapter, value_matrix, adapter_down, adapter_up):
    z_count = lax.axis_size("adapter")
    reqs, steps, width = hidden.shape
    adapters, feats, rank = adapter_down.shape
    columns = adapter_up.shape[2]
    rows, pairs = reqs * steps, adapters // 2
    half = pairs // 2
    down = adapter_down.transpose(0, 2, 1).reshape(pairs, 2 * rank, feats)
    up = adapter_up.reshape(adapters * rank, columns)
    key = jnp.repeat(request_adapter, steps)[:, None] - (jnp.arange(2 * rank, dtype=jnp.int32) // rank)[None, :]
    bf, f32, dma = jnp.bfloat16, jnp.float32, pltpu.SemaphoreType.DMA
    anywhere = pl.BlockSpec(memory_space=pl.ANY)
    whole = pl.BlockSpec(memory_space=pltpu.VMEM)
    return pl.pallas_call(
        functools.partial(kernel, (z_count, pairs, rank, feats)),
        out_shape=jax.ShapeDtypeStruct((reqs, steps, columns), bf),
        in_specs=[anywhere] * 4 + [whole],
        out_specs=whole,
        scratch_shapes=[
            pltpu.VMEM(hidden.shape, bf),
            pltpu.VMEM((rows, width), bf),
            pltpu.VMEM((reqs, steps, feats), bf),
            pltpu.VMEM((rows, feats), bf),
            pltpu.VMEM((rows, 2 * rank), jnp.int32),
            pltpu.VMEM(value_matrix.shape, bf),
            pltpu.VMEM((z_count, half, 2 * rank, feats), bf),
            pltpu.VMEM((z_count, adapters * rank, columns), bf),
            pltpu.VMEM((rows, 2 * rank), f32),
            pltpu.VMEM((rows, 2 * rank), f32),
            pltpu.VMEM((rows, columns), f32),
            pltpu.VMEM((rows, columns), bf),
            pltpu.VMEM((rows, columns), bf),
            pltpu.VMEM((2, rows // 2, 2 * rank), bf),
            pltpu.VMEM((7, rows // 2, 2 * rank), bf),
            pltpu.VMEM((pairs, 2 * rank, feats // 2), bf),
            pltpu.VMEM((reqs, steps, feats // 2), bf),
            pltpu.VMEM((rows, 2 * rank), jnp.int32),
            pltpu.VMEM((rows, 2 * rank), f32),
            pltpu.VMEM((rows // 2, 2 * rank), f32),
            pltpu.VMEM((rows // 2, 2 * rank), bf),
            pltpu.VMEM((rows // 2, 2 * rank), bf),
            dma((3,)),
            dma((3,)),
            dma((5,)),
            dma((2, z_count, half + 1)),
            dma((2, z_count, half + 1)),
            dma((2, z_count)),
            dma((2, z_count)),
            dma((2, z_count)),
            dma((2, z_count)),
            dma((rows // TILE + 1,)),
            dma((rows // TILE + 1,)),
            dma, dma,
            dma((7,)),
            dma((7,)),
        ],
        compiler_params=pltpu.CompilerParams(
            collective_id=0, has_side_effects=True, vmem_limit_bytes=60 * 2 ** 20),
        cost_estimate=pl.CostEstimate(flops=30 * 10 ** 9, bytes_accessed=20 * 10 ** 6, transcendentals=0),
    )(hidden, value_matrix, down, up, key)


def local(hidden, request_adapter, value_matrix, adapter_down, adapter_up):
    z_count = lax.axis_size("adapter")
    reqs, steps, width = hidden.shape
    maps = z_count * (adapter_down.size + adapter_up.size) * 2
    rest = (hidden.size + value_matrix.size) * 2 + reqs * steps * adapter_up.shape[2] * 10
    fits = maps + rest < 50 * 2 ** 20
    if fits and z_count >= 4 and lax.axis_size("tensor") == 2 and lax.axis_size("groups") == 2 and lax.axis_size("sub") == 2:
        return gathered(hidden, request_adapter, value_matrix, adapter_down, adapter_up)
    return routed(hidden, request_adapter, value_matrix, adapter_down, adapter_up)


def solution(mesh):
    return jax.shard_map(
        local,
        mesh=mesh,
        in_specs=(
            P(("groups", "adapter"), None, "tensor"),
            P(("groups", "adapter")),
            P("tensor", "sub"),
            P("adapter", ("tensor", "sub"), None),
            P("adapter", None, "sub"),
        ),
        out_specs=P(("groups", "adapter"), None, "sub"),
        check_vma=False,
    )
```
